512 devices in a mesh: dom: 64 (over x, z, core), col: 8 (over y).
Axes of the slice: x: 4, y: 8, z: 8, core: 2. Of those that a mesh axis runs over, the one named last changes fastest.
Arguments:
- snapshots: bfloat16 [128, 3, 131072], P('col', None, 'dom'), may hold values from -30 to 30
- mass_tiles: bfloat16 [16, 3, 3, 131072], P(None, None, None, 'dom'), may hold values from -2 to 2
- tile_slot: int32 [15, 131072], P(None, 'dom'), may hold values from 0 to 3071
- send_up: int32 [32768], P('dom'), may hold values from 0 to 2047
- send_down: int32 [32768], P('dom'), may hold values from 0 to 2047
Outputs:
- mass_snap: bfloat16 [128, 3, 131072], P('col', None, 'dom')
- gram: float32 [128, 128], P(None, 'col')
The draws below stay inside these ranges and needn't reach their ends.
Inputs may be any that keep to these rules, and one draw needn't show every extreme that they name: `tile_slot`: slots below 2048 are the partition's own nodes, the next 512 those received from the previous partition, the last 512 those from the next partition.
All inputs are finite; a program needn't handle non-finite values.
Results may differ from the reference program's by a relative error of at most 0.001.
Values may be sent and summed in bfloat16 or wider, within the bound.
A program may use at most 64 MiB of HBM per device.

```python
import jax
import jax.numpy as jnp
from jax import lax

NSNAP = 128
TILES = 16
NODES_DEV = 2048
HALO = 512
NODES = 131072
HALO_ALL = 32768
N_DOM = 64


def draw_snapshots(key, part):
    key_common = jax.random.fold_in(key, 11)
    key_fluct = jax.random.fold_in(key, 12)
    key_scale = jax.random.fold_in(key, 13)
    position = jnp.arange(NODES, dtype=jnp.float32) / max(NODES - 1, 1)
    node_weight = 0.6 * jnp.exp(position * jnp.log(3.0))
    common = jnp.clip(jax.random.normal(key_common, (3, NODES), jnp.float32), -4.0, 4.0)
    fluct = jnp.clip(jax.random.normal(key_fluct, (NSNAP, 3, NODES), jnp.float32), -4.0, 4.0)
    snap_scale = jnp.exp(jax.random.uniform(key_scale, (NSNAP, 1, 1), jnp.float32, jnp.log(0.3), jnp.log(3.0)))
    values = node_weight[None, None, :] * (common[None] + snap_scale * fluct)
    return values.astype(jnp.bfloat16)


def draw_mass_tiles(key, part):
    key_off = jax.random.fold_in(key, 21)
    key_diag = jax.random.fold_in(key, 22)
    off_diag = 0.07 * jnp.clip(jax.random.normal(key_off, (TILES, 3, 3, NODES), jnp.float32), -4.0, 4.0)
    diag_vals = jax.random.uniform(key_diag, (3, NODES), jnp.float32, 0.5, 1.5)
    comp_ids = jnp.arange(3)
    identity = (comp_ids[:, None] == comp_ids[None, :]).astype(jnp.float32)
    tile_ids = jnp.arange(TILES)
    first_tile = (tile_ids == 0).astype(jnp.float32)
    values = off_diag + first_tile[:, None, None, None] * identity[None, :, :, None] * diag_vals[None, :, None, :]
    return values.astype(jnp.bfloat16)


def touch_ends(drawn, rng, smallest, largest):
    extent = drawn.shape
    spot = [jax.random.randint(jax.random.fold_in(rng, axis), (), 0, extent[axis]) for axis in range(len(extent))]
    drawn = drawn.at[tuple(spot)].set(smallest)
    longest = extent.index(max(extent))
    spot[longest] = (spot[longest] + 1) % extent[longest]
    return drawn.at[tuple(spot)].set(largest)


def setup_inputs(seed: int = 0) -> dict:
    streams_of = jax.random.split(jax.random.key(seed), 6)
    return {
        "snapshots": draw_snapshots(jax.random.fold_in(streams_of[5], 71), 0),
        "mass_tiles": draw_mass_tiles(jax.random.fold_in(streams_of[5], 71), 0),
        "tile_slot": touch_ends(jax.random.randint(streams_of[2], (TILES - 1, NODES), 0, NODES_DEV + 2 * HALO), jax.random.fold_in(streams_of[2], 1), 0, (NODES_DEV + 2 * HALO) - 1).astype(jnp.int32),
        "send_up": touch_ends(jax.random.randint(streams_of[3], (HALO_ALL,), 0, NODES_DEV), jax.random.fold_in(streams_of[3], 1), 0, NODES_DEV - 1).astype(jnp.int32),
        "send_down": touch_ends(jax.random.randint(streams_of[4], (HALO_ALL,), 0, NODES_DEV), jax.random.fold_in(streams_of[4], 1), 0, NODES_DEV - 1).astype(jnp.int32),
    }


def couple(tiles, values):
    total_sum = tiles[None, :, 0, :].astype(jnp.float32) * values[:, None, 0, :].astype(jnp.float32)
    for in_comp in (1, 2):
        total_sum = total_sum + tiles[None, :, in_comp, :].astype(jnp.float32) * values[:, None, in_comp, :].astype(jnp.float32)
    return total_sum


def reference(snapshots, mass_tiles, tile_slot, send_up, send_down):
    parts = snapshots.reshape(NSNAP, 3, N_DOM, NODES_DEV)
    up_lists = send_up.reshape(N_DOM, HALO)[None, None]
    down_lists = send_down.reshape(N_DOM, HALO)[None, None]
    up_sent = jnp.take_along_axis(parts, up_lists, axis=3)
    down_sent = jnp.take_along_axis(parts, down_lists, axis=3)
    zero_rim = jnp.zeros((NSNAP, 3, 1, HALO), jnp.bfloat16)
    from_lower = jnp.concatenate([zero_rim, up_sent[:, :, :-1]], axis=2)
    from_upper = jnp.concatenate([down_sent[:, :, 1:], zero_rim], axis=2)
    extended = jnp.concatenate([parts, from_lower, from_upper], axis=3)
    slot_parts = tile_slot.reshape(TILES - 1, N_DOM, NODES_DEV)
    first_term = couple(mass_tiles[0], snapshots)

    def add_tile(tile_index, total_sum):
        tiles = lax.dynamic_index_in_dim(mass_tiles, tile_index, 0, keepdims=False)
        slots = lax.dynamic_index_in_dim(slot_parts, tile_index - 1, 0, keepdims=False)
        neighbour_vals = jnp.take_along_axis(extended, slots[None, None], axis=3)
        return total_sum + couple(tiles, neighbour_vals.reshape(NSNAP, 3, NODES))

    mass_snap = lax.fori_loop(1, TILES, add_tile, first_term).astype(jnp.bfloat16)
    flat_snap = snapshots.reshape(NSNAP, 3 * NODES)
    flat_mass = mass_snap.reshape(NSNAP, 3 * NODES)
    gram = lax.dot_general(flat_snap, flat_mass, (((1,), (1,)), ((), ())), preferred_element_type=jnp.float32)
    gram = gram / (3.0 * NODES)
    return mass_snap, gram
```

```python
import functools

import jax
import jax.numpy as jnp
from jax import lax
from jax.experimental import pallas as pl
from jax.experimental.pallas import tpu as pltpu
from jax.sharding import PartitionSpec as P

BF16 = jnp.bfloat16
F32 = jnp.float32
MESH = pl.DeviceIdType.MESH

SNAP = 16
NODES = 2048
BLOCK = 256
OWN = NODES // BLOCK
BLOCKS = 12
OTHERS = 15
COLS = 8
EARLY = 2
LAG = 1


def one_hot(low):
    rows = lax.broadcasted_iota(jnp.int16, (BLOCK, low.shape[1]), 0)
    return jnp.where(rows == low.astype(jnp.int16), jnp.array(1, BF16), jnp.array(0, BF16))


def pick(table, slots, first, count):
    low = slots & (BLOCK - 1)
    high = slots >> 8
    stacked = table[first : first + count].reshape(count * 3 * SNAP, BLOCK)
    products = jnp.dot(stacked, one_hot(low), preferred_element_type=F32)
    found = jnp.zeros((3 * SNAP, slots.shape[1]), F32)
    for block in range(count):
        rows = products[block * 3 * SNAP : (block + 1) * 3 * SNAP]
        found = jnp.where(high == first + block, rows, found)
    return found


def kernel(
    snap_ref,
    tiles_ref,
    slot_ref,
    up_ref,
    down_ref,
    mass_ref,
    gram_ref,
    table,
    early,
    all_snap,
    mass_in,
    part_out,
    part_in,
    z_in,
    xc_in,
    halo_send,
    halo_recv,
    snap_send,
    snap_recv,
    mass_send,
    mass_recv,
    part_send,
    part_recv,
    z_send,
    z_recv,
    xc_send,
    xc_recv,
):
    dom = lax.axis_index("dom")
    col = lax.axis_index("col")
    x_pos = dom // 16
    z_pos = (dom // 2) % 8
    core = dom % 2
    xc_pos = x_pos * 2 + core

    def col_peer(step):
        return (dom, lax.rem(col + step, COLS))

    def z_peer(step):
        return (x_pos * 16 + lax.rem(z_pos + step, 8) * 2 + core, col)

    def xc_peer(step):
        other = lax.rem(xc_pos + step, 8)
        return ((other // 2) * 16 + z_pos * 2 + other % 2, col)

    upper = (lax.rem(dom + 1, 64), col)
    lower = (lax.rem(dom + 63, 64), col)

    barrier = pltpu.get_barrier_semaphore()
    for peer in [upper, lower] + [group(step) for step in range(1, 8) for group in (col_peer, z_peer, xc_peer)]:
        pl.semaphore_signal(barrier, inc=1, device_id=peer, device_id_type=MESH)

    for block in range(OWN):
        table[block] = snap_ref[:, :, block * BLOCK : (block + 1) * BLOCK]
    for side, names in ((0, up_ref), (1, down_ref)):
        shared = pick(table, names[...], 0, OWN).astype(BF16)
        for half in range(2):
            for comp in range(3):
                table[BLOCKS + side * 2 + half, comp] = shared[
                    comp * SNAP : (comp + 1) * SNAP, half * BLOCK : (half + 1) * BLOCK
                ]

    pl.semaphore_wait(barrier, 23)

    halo_copies = []
    for side, peer in ((0, upper), (1, lower)):
        copy = pltpu.make_async_remote_copy(
            src_ref=table.at[pl.ds(BLOCKS + 2 * side, 2)],
            dst_ref=table.at[pl.ds(OWN + 2 * side, 2)],
            send_sem=halo_send.at[side],
            recv_sem=halo_recv.at[side],
            device_id=peer,
            device_id_type=MESH,
        )
        copy.start()
        halo_copies.append(copy)
    snap_copies = []
    for step in range(1, COLS):
        target = lax.rem(col + step, COLS)
        copy = pltpu.make_async_remote_copy(
            src_ref=snap_ref.at[:, :, pl.ds(pl.multiple_of(target * BLOCK, BLOCK), BLOCK)],
            dst_ref=all_snap.at[:, pl.ds(pl.multiple_of(col * SNAP, SNAP), SNAP), :],
            send_sem=snap_send.at[step - 1],
            recv_sem=snap_recv.at[step - 1],
            device_id=(dom, target),
            device_id_type=MESH,
        )
        copy.start()
        snap_copies.append(copy)
    all_snap[:, pl.ds(pl.multiple_of(col * SNAP, SNAP), SNAP), :] = table[col]

    def chunk_of(step):
        return lax.rem(col + 1 + step, COLS)

    def columns_of(chunk):
        return pl.ds(pl.multiple_of(chunk * BLOCK, BLOCK), BLOCK)

    def tile_sums(columns, total, own_values, first, count):
        coefs = [[tiles_ref[a, b, :, columns].astype(F32) for b in range(3)] for a in range(3)]
        if own_values is not None:
            for a in range(3):
                for b in range(3):
                    total[a] = total[a] + coefs[a][b][0:1] * own_values[b]
        slots = slot_ref[:, columns]
        for start in range(0, OTHERS, 2):
            ks = range(start, min(start + 2, OTHERS))
            found = pick(table, jnp.concatenate([slots[k : k + 1] for k in ks], axis=1), first, count)
            for place, k in enumerate(ks):
                for a in range(3):
                    for b in range(3):
                        values = found[b * SNAP : (b + 1) * SNAP, place * BLOCK : (place + 1) * BLOCK]
                        total[a] = total[a] + coefs[a][b][k + 1 : k + 2] * values
        return total

    def zeros():
        return [jnp.zeros((SNAP, BLOCK), F32) for _ in range(3)]

    def early_step(step, carry):
        chunk = chunk_of(step)
        total = tile_sums(columns_of(chunk), zeros(), table[chunk].astype(F32), 0, OWN)
        for a in range(3):
            early[step, a] = total[a]
        return carry

    lax.fori_loop(0, EARLY, early_step, 0)

    for copy in halo_copies:
        copy.wait_recv()

    @pl.when(dom == 0)
    def _():
        table[OWN : OWN + 2] = jnp.zeros((2, 3, SNAP, BLOCK), BF16)

    @pl.when(dom == 63)
    def _():
        table[OWN + 2 : OWN + 4] = jnp.zeros((2, 3, SNAP, BLOCK), BF16)

    def mass_copy(step):
        chunk = chunk_of(step)
        return pltpu.make_async_remote_copy(
            src_ref=mass_ref.at[:, :, columns_of(chunk)],
            dst_ref=mass_in.at[step],
            send_sem=mass_send.at[step],
            recv_sem=mass_recv.at[step],
            device_id=(dom, chunk),
            device_id_type=MESH,
        )

    def part_copy(step):
        return pltpu.make_async_remote_copy(
            src_ref=part_out.at[step],
            dst_ref=part_in.at[step],
            send_sem=part_send.at[step],
            recv_sem=part_recv.at[step],
            device_id=(dom, lax.rem(col + 7 - step, COLS)),
            device_id_type=MESH,
        )

    def products(rows):
        total = None
        for a in range(3):
            term = lax.dot_general(
                rows[a], all_snap[a], (((1,), (1,)), ((), ())), preferred_element_type=F32
            )
            total = term if total is None else total + term
        return total

    def finish(step, total):
        columns = columns_of(chunk_of(step))
        for a in range(3):
            mass_ref[a, :, columns] = total[a].astype(BF16)

        @pl.when(step < COLS - 1)
        def _():
            mass_copy(step).start()

    def answer(step):
        mass_copy(step).wait_recv()
        part_out[step] = products(mass_in[step])
        part_copy(step).start()

    def late_step(step, carry):
        columns = columns_of(chunk_of(step))
        total = tile_sums(columns, [early[step, a] for a in range(3)], None, OWN, BLOCKS - OWN)
        finish(step, total)
        return carry

    lax.fori_loop(0, EARLY, late_step, 0)

    for copy in snap_copies:
        copy.wait_recv()

    def full_step(step, carry):
        chunk = chunk_of(step)
        total = tile_sums(columns_of(chunk), zeros(), table[chunk].astype(F32), 0, BLOCKS)
        finish(step, total)
        answer(step - LAG)
        return carry

    for step in range(EARLY - LAG):
        answer(jnp.int32(step))
    lax.fori_loop(EARLY, COLS, full_step, 0)
    for step in range(COLS - LAG, COLS - 1):
        answer(jnp.int32(step))

    own_part = products(mass_ref[:, :, columns_of(col)])
    for step in range(COLS - 1):
        part_copy(step).wait_recv()
        own_part = own_part + part_in[step]

    def exchange(value, place, slots, peer_of, sends, recvs):
        slots[place] = value
        copies = []
        for step in range(1, 8):
            copy = pltpu.make_async_remote_copy(
                src_ref=slots.at[place],
                dst_ref=slots.at[place],
                send_sem=sends.at[step - 1],
                recv_sem=recvs.at[step - 1],
                device_id=peer_of(step),
                device_id_type=MESH,
            )
            copy.start()
            copies.append(copy)
        for copy in copies:
            copy.wait_recv()
        total = slots[0]
        for other in range(1, 8):
            total = total + slots[other]
        return total, copies

    z_sum, z_copies = exchange(own_part, z_pos, z_in, z_peer, z_send, z_recv)
    xc_sum, xc_copies = exchange(z_sum, xc_pos, xc_in, xc_peer, xc_send, xc_recv)
    gram_ref[...] = xc_sum / (3.0 * NODES * 64)

    for copy in halo_copies + snap_copies + z_copies + xc_copies:
        copy.wait_send()
    for step in range(COLS - 1):
        mass_copy(step).wait_send()
        part_copy(step).wait_send()


def body(snapshots, mass_tiles, tile_slot, send_up, send_down):
    vmem = pl.BlockSpec(memory_space=pltpu.VMEM)
    dma = pltpu.SemaphoreType.DMA
    mass, gram = pl.pallas_call(
        kernel,
        out_shape=(
            jax.ShapeDtypeStruct((3, SNAP, NODES), BF16),
            jax.ShapeDtypeStruct((SNAP, COLS * SNAP), F32),
        ),
        in_specs=[vmem] * 5,
        out_specs=(vmem, vmem),
        scratch_shapes=[
            pltpu.VMEM((BLOCKS + 4, 3, SNAP, BLOCK), BF16),
            pltpu.VMEM((EARLY, 3, SNAP, BLOCK), F32),
            pltpu.VMEM((3, COLS * SNAP, BLOCK), BF16),
            pltpu.VMEM((COLS - 1, 3, SNAP, BLOCK), BF16),
            pltpu.VMEM((COLS - 1, SNAP, COLS * SNAP), F32),
            pltpu.VMEM((COLS - 1, SNAP, COLS * SNAP), F32),
            pltpu.VMEM((8, SNAP, COLS * SNAP), F32),
            pltpu.VMEM((8, SNAP, COLS * SNAP), F32),
            dma((2,)),
            dma((2,)),
        ]
        + [dma((7,))] * 10,
        compiler_params=pltpu.CompilerParams(
            collective_id=0, has_side_effects=True, vmem_limit_bytes=32 * 2**20
        ),
        cost_estimate=pl.CostEstimate(flops=9_100_000_000, bytes_accessed=1_200_000, transcendentals=0),
    )(
        jnp.transpose(snapshots, (1, 0, 2)),
        jnp.transpose(mass_tiles, (1, 2, 0, 3)),
        tile_slot,
        send_up.reshape(1, -1),
        send_down.reshape(1, -1),
    )
    return jnp.transpose(mass, (1, 0, 2)), jnp.transpose(gram, (1, 0))


def solution(mesh):
    placed = (P("col", None, "dom"), P(None, None, None, "dom"), P(None, "dom"), P("dom"), P("dom"))
    return jax.shard_map(
        body,
        mesh=mesh,
        in_specs=placed,
        out_specs=(P("col", None, "dom"), P(None, "col")),
        check_vma=False,
    )
```

```python
import functools

import jax
import jax.numpy as jnp
from jax import lax
from jax.experimental import pallas as pl
from jax.experimental.pallas import tpu as pltpu
from jax.sharding import PartitionSpec as P

BF16 = jnp.bfloat16
F32 = jnp.float32
MESH = pl.DeviceIdType.MESH

SNAP = 16
NODES = 2048
BLOCK = 256
OWN = NODES // BLOCK
BLOCKS = 12
OTHERS = 15
COLS = 8
BEFORE = 2
EARLY = 4
FIRST_ANSWERS = 5


def one_hot(low):
    rows = lax.broadcasted_iota(jnp.int16, (BLOCK, low.shape[1]), 0)
    return jnp.where(rows == low.astype(jnp.int16), jnp.array(1, BF16), jnp.array(0, BF16))


def pick(table, slots, first, count):
    low = slots & (BLOCK - 1)
    high = slots >> 8
    stacked = table[first : first + count].reshape(count * 3 * SNAP, BLOCK)
    products = jnp.dot(stacked, one_hot(low), preferred_element_type=F32)
    found = jnp.zeros((3 * SNAP, slots.shape[1]), F32)
    for block in range(count):
        rows = products[block * 3 * SNAP : (block + 1) * 3 * SNAP]
        found = jnp.where(high == first + block, rows, found)
    return found


def kernel(
    snap_hbm,
    tiles_hbm,
    slot_hbm,
    up_hbm,
    down_hbm,
    mass_ref,
    gram_ref,
    table,
    tiles_ref,
    slot_ref,
    up_ref,
    down_ref,
    early,
    all_snap,
    mass_in,
    part_out,
    part_in,
    z_in,
    xc_in,
    load_snap,
    load_rest,
    halo_send,
    halo_recv,
    snap_send,
    snap_recv,
    mass_send,
    mass_recv,
    part_send,
    part_recv,
    z_send,
    z_recv,
    xc_send,
    xc_recv,
):
    dom = lax.axis_index("dom")
    col = lax.axis_index("col")
    x_pos = dom // 16
    z_pos = (dom // 2) % 8
    core = dom % 2
    xc_pos = x_pos * 2 + core

    def col_peer(step):
        return (dom, lax.rem(col + step, COLS))

    def z_peer(step):
        return (x_pos * 16 + lax.rem(z_pos + step, 8) * 2 + core, col)

    def xc_peer(step):
        other = lax.rem(xc_pos + step, 8)
        return ((other // 2) * 16 + z_pos * 2 + other % 2, col)

    upper = (lax.rem(dom + 1, 64), col)
    lower = (lax.rem(dom + 63, 64), col)

    snap_loads = [
        pltpu.make_async_copy(
            snap_hbm.at[:, :, pl.ds(block * BLOCK, BLOCK)], table.at[block], load_snap.at[block]
        )
        for block in range(OWN)
    ]
    name_loads = [
        pltpu.make_async_copy(up_hbm, up_ref, load_rest.at[0]),
        pltpu.make_async_copy(down_hbm, down_ref, load_rest.at[1]),
    ]
    tile_loads = [
        pltpu.make_async_copy(slot_hbm, slot_ref, load_rest.at[2]),
        pltpu.make_async_copy(tiles_hbm, tiles_ref, load_rest.at[3]),
    ]
    for load in name_loads + snap_loads + tile_loads:
        load.start()

    barrier = pltpu.get_barrier_semaphore()
    for peer in [upper, lower] + [group(step) for step in range(1, 8) for group in (col_peer, z_peer, xc_peer)]:
        pl.semaphore_signal(barrier, inc=1, device_id=peer, device_id_type=MESH)

    for load in name_loads + snap_loads:
        load.wait()
    for side, names in ((0, up_ref), (1, down_ref)):
        shared = pick(table, names[...], 0, OWN).astype(BF16)
        for half in range(2):
            for comp in range(3):
                table[BLOCKS + side * 2 + half, comp] = shared[
                    comp * SNAP : (comp + 1) * SNAP, half * BLOCK : (half + 1) * BLOCK
                ]

    def offset_of(step):
        return 4 + (1 - 2 * lax.rem(step, 2)) * lax.div(step + 1, 2)

    def chunk_of(step):
        return lax.rem(col + offset_of(step), COLS)

    def columns_of(chunk):
        return pl.ds(pl.multiple_of(chunk * BLOCK, BLOCK), BLOCK)

    def tile_sums(columns, total, own_values, first, count):
        coefs = [[tiles_ref[a, b, :, columns].astype(F32) for b in range(3)] for a in range(3)]
        if own_values is not None:
            for a in range(3):
                for b in range(3):
                    total[a] = total[a] + coefs[a][b][0:1] * own_values[b]
        slots = slot_ref[:, columns]
        for start in range(0, OTHERS, 2):
            ks = range(start, min(start + 2, OTHERS))
            found = pick(table, jnp.concatenate([slots[k : k + 1] for k in ks], axis=1), first, count)
            for place, k in enumerate(ks):
                for a in range(3):
                    for b in range(3):
                        values = found[b * SNAP : (b + 1) * SNAP, place * BLOCK : (place + 1) * BLOCK]
                        total[a] = total[a] + coefs[a][b][k + 1 : k + 2] * values
        return total

    def zeros():
        return [jnp.zeros((SNAP, BLOCK), F32) for _ in range(3)]

    def early_step(step, carry):
        chunk = chunk_of(step)
        total = tile_sums(columns_of(chunk), zeros(), table[chunk].astype(F32), 0, OWN)
        for a in range(3):
            early[step, a] = total[a]
        return carry

    for load in tile_loads:
        load.wait()
    lax.fori_loop(0, BEFORE, early_step, 0)

    pl.semaphore_wait(barrier, 23)

    halo_copies = []
    for side, peer in ((0, upper), (1, lower)):
        copy = pltpu.make_async_remote_copy(
            src_ref=table.at[pl.ds(BLOCKS + 2 * side, 2)],
            dst_ref=table.at[pl.ds(OWN + 2 * side, 2)],
            send_sem=halo_send.at[side],
            recv_sem=halo_recv.at[side],
            device_id=peer,
            device_id_type=MESH,
        )
        copy.start()
        halo_copies.append(copy)
    snap_copies = []
    for step in range(1, COLS):
        target = lax.rem(col + step, COLS)
        copy = pltpu.make_async_remote_copy(
            src_ref=table.at[target],
            dst_ref=all_snap.at[:, pl.ds(pl.multiple_of(col * SNAP, SNAP), SNAP), :],
            send_sem=snap_send.at[step - 1],
            recv_sem=snap_recv.at[step - 1],
            device_id=(dom, target),
            device_id_type=MESH,
        )
        copy.start()
        snap_copies.append(copy)
    all_snap[:, pl.ds(pl.multiple_of(col * SNAP, SNAP), SNAP), :] = table[col]

    lax.fori_loop(BEFORE, EARLY, early_step, 0)

    for copy in halo_copies:
        copy.wait_recv()

    @pl.when(dom == 0)
    def _():
        table[OWN : OWN + 2] = jnp.zeros((2, 3, SNAP, BLOCK), BF16)

    @pl.when(dom == 63)
    def _():
        table[OWN + 2 : OWN + 4] = jnp.zeros((2, 3, SNAP, BLOCK), BF16)

    def mass_copy(step):
        chunk = chunk_of(step)
        return pltpu.make_async_remote_copy(
            src_ref=mass_ref.at[:, :, columns_of(chunk)],
            dst_ref=mass_in.at[step],
            send_sem=mass_send.at[step],
            recv_sem=mass_recv.at[step],
            device_id=(dom, chunk),
            device_id_type=MESH,
        )

    def part_copy(step):
        return pltpu.make_async_remote_copy(
            src_ref=part_out.at[step],
            dst_ref=part_in.at[step],
            send_sem=part_send.at[step],
            recv_sem=part_recv.at[step],
            device_id=(dom, lax.rem(col + COLS - offset_of(step), COLS)),
            device_id_type=MESH,
        )

    def products(first, last):
        total = None
        for a in range(3):
            rows = mass_in[first:last, a].reshape((last - first) * SNAP, BLOCK)
            term = lax.dot_general(rows, all_snap[a], (((1,), (1,)), ((), ())), preferred_element_type=F32)
            total = term if total is None else total + term
        return total

    def finish(step, total):
        columns = columns_of(chunk_of(step))
        for a in range(3):
            mass_ref[a, :, columns] = total[a].astype(BF16)

        @pl.when(step < COLS - 1)
        def _():
            mass_copy(step).start()

    def answer(first, last, also_own):
        for step in range(first, last):
            mass_copy(step).wait_recv()
        total = products(first, last + 1 if also_own else last)
        for step in range(first, last):
            part_out[step] = total[(step - first) * SNAP : (step - first + 1) * SNAP]
            part_copy(step).start()
        return total[(last - first) * SNAP :]

    def late_step(step, carry):
        columns = columns_of(chunk_of(step))
        total = tile_sums(columns, [early[step, a] for a in range(3)], None, OWN, BLOCKS - OWN)
        finish(step, total)
        return carry

    lax.fori_loop(0, EARLY, late_step, 0)

    def full_step(step, carry):
        chunk = chunk_of(step)
        total = tile_sums(columns_of(chunk), zeros(), table[chunk].astype(F32), 0, BLOCKS)
        finish(step, total)

        @pl.when(step == COLS - 2)
        def _():
            for copy in snap_copies:
                copy.wait_recv()
            answer(0, FIRST_ANSWERS, False)

        return carry

    lax.fori_loop(EARLY, COLS, full_step, 0)

    mass_in[COLS - 1] = mass_ref[:, :, columns_of(col)]
    own_part = answer(FIRST_ANSWERS, COLS - 1, True)
    for step in range(COLS - 1):
        part_copy(step).wait_recv()
        own_part = own_part + part_in[step]

    def exchange(value, place, slots, peer_of, sends, recvs):
        slots[place] = value
        copies = []
        for step in range(1, 8):
            copy = pltpu.make_async_remote_copy(
                src_ref=slots.at[place],
                dst_ref=slots.at[place],
                send_sem=sends.at[step - 1],
                recv_sem=recvs.at[step - 1],
                device_id=peer_of(step),
                device_id_type=MESH,
            )
            copy.start()
            copies.append(copy)
        for copy in copies:
            copy.wait_recv()
        total = slots[0]
        for other in range(1, 8):
            total = total + slots[other]
        return total, copies

    z_sum, z_copies = exchange(own_part, z_pos, z_in, z_peer, z_send, z_recv)
    xc_sum, xc_copies = exchange(z_sum, xc_pos, xc_in, xc_peer, xc_send, xc_recv)
    gram_ref[...] = xc_sum / (3.0 * NODES * 64)

    for copy in halo_copies + snap_copies + z_copies + xc_copies:
        copy.wait_send()
    for step in range(COLS - 1):
        mass_copy(step).wait_send()
        part_copy(step).wait_send()


def body(snapshots, mass_tiles, tile_slot, send_up, send_down):
    vmem = pl.BlockSpec(memory_space=pltpu.VMEM)
    dma = pltpu.SemaphoreType.DMA
    mass, gram = pl.pallas_call(
        kernel,
        out_shape=(
            jax.ShapeDtypeStruct((3, SNAP, NODES), BF16),
            jax.ShapeDtypeStruct((SNAP, COLS * SNAP), F32),
        ),
        in_specs=[pl.BlockSpec(memory_space=pltpu.HBM)] * 5,
        out_specs=(vmem, vmem),
        scratch_shapes=[
            pltpu.VMEM((BLOCKS + 4, 3, SNAP, BLOCK), BF16),
            pltpu.VMEM((3, 3, OTHERS + 1, NODES), BF16),
            pltpu.VMEM((OTHERS, NODES), jnp.int32),
            pltpu.VMEM((1, 2 * BLOCK), jnp.int32),
            pltpu.VMEM((1, 2 * BLOCK), jnp.int32),
            pltpu.VMEM((EARLY, 3, SNAP, BLOCK), F32),
            pltpu.VMEM((3, COLS * SNAP, BLOCK), BF16),
            pltpu.VMEM((COLS, 3, SNAP, BLOCK), BF16),
            pltpu.VMEM((COLS - 1, SNAP, COLS * SNAP), F32),
            pltpu.VMEM((COLS - 1, SNAP, COLS * SNAP), F32),
            pltpu.VMEM((8, SNAP, COLS * SNAP), F32),
            pltpu.VMEM((8, SNAP, COLS * SNAP), F32),
            dma((OWN,)),
            dma((4,)),
            dma((2,)),
            dma((2,)),
        ]
        + [dma((7,))] * 10,
        compiler_params=pltpu.CompilerParams(
            collective_id=0, has_side_effects=True, vmem_limit_bytes=32 * 2**20
        ),
        cost_estimate=pl.CostEstimate(flops=9_100_000_000, bytes_accessed=1_200_000, transcendentals=0),
    )(
        *(
            pltpu.with_memory_space_constraint(operand, pltpu.HBM)
            for operand in (
                jnp.transpose(snapshots, (1, 0, 2)),
                jnp.transpose(mass_tiles, (1, 2, 0, 3)),
                tile_slot,
                send_up.reshape(1, -1),
                send_down.reshape(1, -1),
            )
        )
    )
    return jnp.transpose(mass, (1, 0, 2)), jnp.transpose(gram, (1, 0))


def solution(mesh):
    placed = (P("col", None, "dom"), P(None, None, None, "dom"), P(None, "dom"), P("dom"), P("dom"))
    return jax.shard_map(
        body,
        mesh=mesh,
        in_specs=placed,
        out_specs=(P("col", None, "dom"), P(None, "col")),
        check_vma=False,
    )
```

```python
import functools

import jax
import jax.numpy as jnp
from jax import lax
from jax.experimental import pallas as pl
from jax.experimental.pallas import tpu as pltpu
from jax.sharding import PartitionSpec as P

BF16 = jnp.bfloat16
F32 = jnp.float32
MESH = pl.DeviceIdType.MESH

SNAP = 16
NODES = 2048
BLOCK = 256
OWN = NODES // BLOCK
BLOCKS = 12
OTHERS = 15
COLS = 8
BEFORE = 2
EARLY = 4
FAR_FIRST = (4, 3, 5, 2, 6, 1, 7)
FIRST_ANSWERS = 5


def one_hot(low):
    rows = lax.broadcasted_iota(jnp.int16, (BLOCK, low.shape[1]), 0)
    return jnp.where(rows == low.astype(jnp.int16), jnp.array(1, BF16), jnp.array(0, BF16))


def pick(table, slots, first, count):
    low = slots & (BLOCK - 1)
    high = slots >> 8
    stacked = table[first : first + count].reshape(count * 3 * SNAP, BLOCK)
    products = jnp.dot(stacked, one_hot(low), preferred_element_type=F32)
    found = jnp.zeros((3 * SNAP, slots.shape[1]), F32)
    for block in range(count):
        rows = products[block * 3 * SNAP : (block + 1) * 3 * SNAP]
        found = jnp.where(high == first + block, rows, found)
    return found


def kernel(
    snap_hbm,
    tiles_hbm,
    slot_hbm,
    up_hbm,
    down_hbm,
    mass_ref,
    gram_ref,
    table,
    tiles_ref,
    slot_ref,
    up_ref,
    down_ref,
    early,
    all_snap,
    mass_in,
    part_out,
    part_in,
    z_in,
    xc_in,
    load_snap,
    load_rest,
    halo_send,
    halo_recv,
    snap_send,
    snap_recv,
    mass_send,
    mass_recv,
    part_send,
    part_recv,
    z_send,
    z_recv,
    xc_send,
    xc_recv,
):
    dom = lax.axis_index("dom")
    col = lax.axis_index("col")
    x_pos = dom // 16
    z_pos = (dom // 2) % 8
    core = dom % 2
    xc_pos = x_pos * 2 + core

    def col_peer(step):
        return (dom, lax.rem(col + step, COLS))

    def z_peer(step):
        return (x_pos * 16 + lax.rem(z_pos + step, 8) * 2 + core, col)

    def xc_peer(step):
        other = lax.rem(xc_pos + step, 8)
        return ((other // 2) * 16 + z_pos * 2 + other % 2, col)

    upper = (lax.rem(dom + 1, 64), col)
    lower = (lax.rem(dom + 63, 64), col)

    snap_loads = [
        pltpu.make_async_copy(
            snap_hbm.at[:, :, pl.ds(block * BLOCK, BLOCK)], table.at[block], load_snap.at[block]
        )
        for block in range(OWN)
    ]
    name_loads = [
        pltpu.make_async_copy(up_hbm, up_ref, load_rest.at[0]),
        pltpu.make_async_copy(down_hbm, down_ref, load_rest.at[1]),
    ]
    tile_loads = [
        pltpu.make_async_copy(slot_hbm, slot_ref, load_rest.at[2]),
        pltpu.make_async_copy(tiles_hbm, tiles_ref, load_rest.at[3]),
    ]
    for load in name_loads + snap_loads + tile_loads:
        load.start()

    barrier = pltpu.get_barrier_semaphore()
    for peer in [group(step) for group in (col_peer, z_peer, xc_peer) for step in FAR_FIRST] + [upper, lower]:
        pl.semaphore_signal(barrier, inc=1, device_id=peer, device_id_type=MESH)

    for load in name_loads + snap_loads:
        load.wait()
    for side, names in ((0, up_ref), (1, down_ref)):
        shared = pick(table, names[...], 0, OWN).astype(BF16)
        for half in range(2):
            for comp in range(3):
                table[BLOCKS + side * 2 + half, comp] = shared[
                    comp * SNAP : (comp + 1) * SNAP, half * BLOCK : (half + 1) * BLOCK
                ]

    def offset_of(step):
        return 4 + (1 - 2 * lax.rem(step, 2)) * lax.div(step + 1, 2)

    def chunk_of(step):
        return lax.rem(col + offset_of(step), COLS)

    def columns_of(chunk):
        return pl.ds(pl.multiple_of(chunk * BLOCK, BLOCK), BLOCK)

    def tile_sums(columns, total, own_values, first, count):
        coefs = [[tiles_ref[a, b, :, columns].astype(F32) for b in range(3)] for a in range(3)]
        if own_values is not None:
            for a in range(3):
                for b in range(3):
                    total[a] = total[a] + coefs[a][b][0:1] * own_values[b]
        slots = slot_ref[:, columns]
        for start in range(0, OTHERS, 2):
            ks = range(start, min(start + 2, OTHERS))
            found = pick(table, jnp.concatenate([slots[k : k + 1] for k in ks], axis=1), first, count)
            for place, k in enumerate(ks):
                for a in range(3):
                    for b in range(3):
                        values = found[b * SNAP : (b + 1) * SNAP, place * BLOCK : (place + 1) * BLOCK]
                        total[a] = total[a] + coefs[a][b][k + 1 : k + 2] * values
        return total

    def zeros():
        return [jnp.zeros((SNAP, BLOCK), F32) for _ in range(3)]

    def early_step(step, carry):
        chunk = chunk_of(step)
        total = tile_sums(columns_of(chunk), zeros(), table[chunk].astype(F32), 0, OWN)
        for a in range(3):
            early[step, a] = total[a]
        return carry

    for load in tile_loads:
        load.wait()
    def halo_copy(side):
        return pltpu.make_async_remote_copy(
            src_ref=table.at[pl.ds(BLOCKS + 2 * side, 2)],
            dst_ref=table.at[pl.ds(OWN + 2 * side, 2)],
            send_sem=halo_send.at[side],
            recv_sem=halo_recv.at[side],
            device_id=(upper, lower)[side],
            device_id_type=MESH,
        )

    def snap_copy(step):
        target = lax.rem(col + step, COLS)
        return pltpu.make_async_remote_copy(
            src_ref=table.at[target],
            dst_ref=all_snap.at[:, pl.ds(pl.multiple_of(col * SNAP, SNAP), SNAP), :],
            send_sem=snap_send.at[step - 1],
            recv_sem=snap_recv.at[step - 1],
            device_id=(dom, target),
            device_id_type=MESH,
        )

    def early_and_send(step, carry):
        early_step(step, carry)

        @pl.when(step == BEFORE - 1)
        def _():
            pl.semaphore_wait(barrier, 23)
            for side in range(2):
                halo_copy(side).start()
            for peer_step in FAR_FIRST:
                snap_copy(peer_step).start()
            all_snap[:, pl.ds(pl.multiple_of(col * SNAP, SNAP), SNAP), :] = table[col]

        return carry

    lax.fori_loop(0, EARLY, early_and_send, 0)

    for side in range(2):
        halo_copy(side).wait_recv()

    @pl.when(dom == 0)
    def _():
        table[OWN : OWN + 2] = jnp.zeros((2, 3, SNAP, BLOCK), BF16)

    @pl.when(dom == 63)
    def _():
        table[OWN + 2 : OWN + 4] = jnp.zeros((2, 3, SNAP, BLOCK), BF16)

    def mass_copy(step):
        chunk = chunk_of(step)
        return pltpu.make_async_remote_copy(
            src_ref=mass_ref.at[:, :, columns_of(chunk)],
            dst_ref=mass_in.at[step],
            send_sem=mass_send.at[step],
            recv_sem=mass_recv.at[step],
            device_id=(dom, chunk),
            device_id_type=MESH,
        )

    def part_copy(step):
        return pltpu.make_async_remote_copy(
            src_ref=part_out.at[step],
            dst_ref=part_in.at[step],
            send_sem=part_send.at[step],
            recv_sem=part_recv.at[step],
            device_id=(dom, lax.rem(col + COLS - offset_of(step), COLS)),
            device_id_type=MESH,
        )

    def products(first, last):
        total = None
        for a in range(3):
            rows = mass_in[first:last, a].reshape((last - first) * SNAP, BLOCK)
            term = lax.dot_general(rows, all_snap[a], (((1,), (1,)), ((), ())), preferred_element_type=F32)
            total = term if total is None else total + term
        return total

    def finish(step, total):
        columns = columns_of(chunk_of(step))
        for a in range(3):
            mass_ref[a, :, columns] = total[a].astype(BF16)

        @pl.when(step < COLS - 1)
        def _():
            mass_copy(step).start()

    def answer(first, last, also_own):
        for step in range(first, last):
            mass_copy(step).wait_recv()
        total = products(first, last + 1 if also_own else last)
        for step in range(first, last):
            part_out[step] = total[(step - first) * SNAP : (step - first + 1) * SNAP]
            part_copy(step).start()
        return total[(last - first) * SNAP :]

    def late_step(step, carry):
        columns = columns_of(chunk_of(step))
        total = tile_sums(columns, [early[step, a] for a in range(3)], None, OWN, BLOCKS - OWN)
        finish(step, total)
        return carry

    lax.fori_loop(0, EARLY, late_step, 0)

    def full_step(step, carry):
        chunk = chunk_of(step)
        total = tile_sums(columns_of(chunk), zeros(), table[chunk].astype(F32), 0, BLOCKS)
        finish(step, total)

        @pl.when(step == COLS - 2)
        def _():
            for peer_step in FAR_FIRST:
                snap_copy(peer_step).wait_recv()
            answer(0, FIRST_ANSWERS, False)

        return carry

    lax.fori_loop(EARLY, COLS, full_step, 0)

    mass_in[COLS - 1] = mass_ref[:, :, columns_of(col)]
    own_part = answer(FIRST_ANSWERS, COLS - 1, True)
    for step in range(COLS - 1):
        part_copy(step).wait_recv()
        own_part = own_part + part_in[step]

    def exchange(value, place, slots, peer_of, sends, recvs):
        slots[place] = value
        copies = []
        for step in FAR_FIRST:
            copy = pltpu.make_async_remote_copy(
                src_ref=slots.at[place],
                dst_ref=slots.at[place],
                send_sem=sends.at[step - 1],
                recv_sem=recvs.at[step - 1],
                device_id=peer_of(step),
                device_id_type=MESH,
            )
            copy.start()
            copies.append(copy)
        for copy in copies:
            copy.wait_recv()
        total = slots[0]
        for other in range(1, 8):
            total = total + slots[other]
        return total, copies

    z_sum, z_copies = exchange(own_part, z_pos, z_in, z_peer, z_send, z_recv)
    xc_sum, xc_copies = exchange(z_sum, xc_pos, xc_in, xc_peer, xc_send, xc_recv)
    gram_ref[...] = xc_sum / (3.0 * NODES * 64)

    for copy in z_copies + xc_copies:
        copy.wait_send()
    for side in range(2):
        halo_copy(side).wait_send()
    for peer_step in FAR_FIRST:
        snap_copy(peer_step).wait_send()
    for step in range(COLS - 1):
        mass_copy(step).wait_send()
        part_copy(step).wait_send()


def body(snapshots, mass_tiles, tile_slot, send_up, send_down):
    vmem = pl.BlockSpec(memory_space=pltpu.VMEM)
    dma = pltpu.SemaphoreType.DMA
    mass, gram = pl.pallas_call(
        kernel,
        out_shape=(
            jax.ShapeDtypeStruct((3, SNAP, NODES), BF16),
            jax.ShapeDtypeStruct((SNAP, COLS * SNAP), F32),
        ),
        in_specs=[pl.BlockSpec(memory_space=pltpu.HBM)] * 5,
        out_specs=(vmem, vmem),
        scratch_shapes=[
            pltpu.VMEM((BLOCKS + 4, 3, SNAP, BLOCK), BF16),
            pltpu.VMEM((3, 3, OTHERS + 1, NODES), BF16),
            pltpu.VMEM((OTHERS, NODES), jnp.int32),
            pltpu.VMEM((1, 2 * BLOCK), jnp.int32),
            pltpu.VMEM((1, 2 * BLOCK), jnp.int32),
            pltpu.VMEM((EARLY, 3, SNAP, BLOCK), F32),
            pltpu.VMEM((3, COLS * SNAP, BLOCK), BF16),
            pltpu.VMEM((COLS, 3, SNAP, BLOCK), BF16),
            pltpu.VMEM((COLS - 1, SNAP, COLS * SNAP), F32),
            pltpu.VMEM((COLS - 1, SNAP, COLS * SNAP), F32),
            pltpu.VMEM((8, SNAP, COLS * SNAP), F32),
            pltpu.VMEM((8, SNAP, COLS * SNAP), F32),
            dma((OWN,)),
            dma((4,)),
            dma((2,)),
            dma((2,)),
        ]
        + [dma((7,))] * 10,
        compiler_params=pltpu.CompilerParams(
            collective_id=0, has_side_effects=True, vmem_limit_bytes=32 * 2**20
        ),
        cost_estimate=pl.CostEstimate(flops=9_100_000_000, bytes_accessed=1_200_000, transcendentals=0),
    )(
        *(
            pltpu.with_memory_space_constraint(operand, pltpu.HBM)
            for operand in (
                jnp.transpose(snapshots, (1, 0, 2)),
                jnp.transpose(mass_tiles, (1, 2, 0, 3)),
                tile_slot,
                send_up.reshape(1, -1),
                send_down.reshape(1, -1),
            )
        )
    )
    return jnp.transpose(mass, (1, 0, 2)), jnp.transpose(gram, (1, 0))


def solution(mesh):
    placed = (P("col", None, "dom"), P(None, None, None, "dom"), P(None, "dom"), P("dom"), P("dom"))
    return jax.shard_map(
        body,
        mesh=mesh,
        in_specs=placed,
        out_specs=(P("col", None, "dom"), P(None, "col")),
        check_vma=False,
    )
```

```python
import functools

import jax
import jax.numpy as jnp
from jax import lax
from jax.experimental import pallas as pl
from jax.experimental.pallas import tpu as pltpu
from jax.sharding import PartitionSpec as P

BF16 = jnp.bfloat16
F32 = jnp.float32
MESH = pl.DeviceIdType.MESH

SNAP = 16
NODES = 2048
BLOCK = 256
OWN = NODES // BLOCK
BLOCKS = 12
OTHERS = 15
COLS = 8
BEFORE = 2
EARLY = 4
FAR_FIRST = (4, 3, 5, 2, 6, 1, 7)
X_STEPS = (2, 1, 3)
FIRST_ANSWERS = 5


def one_hot(low):
    rows = lax.broadcasted_iota(jnp.int16, (BLOCK, low.shape[1]), 0)
    return jnp.where(rows == low.astype(jnp.int16), jnp.array(1, BF16), jnp.array(0, BF16))


def pick(table, slots, first, count):
    low = slots & (BLOCK - 1)
    high = slots >> 8
    stacked = table[first : first + count].reshape(count * 3 * SNAP, BLOCK)
    products = jnp.dot(stacked, one_hot(low), preferred_element_type=F32)
    found = jnp.zeros((3 * SNAP, slots.shape[1]), F32)
    for block in range(count):
        rows = products[block * 3 * SNAP : (block + 1) * 3 * SNAP]
        found = jnp.where(high == first + block, rows, found)
    return found


def kernel(
    snap_hbm,
    tiles_hbm,
    slot_hbm,
    up_hbm,
    down_hbm,
    mass_ref,
    gram_ref,
    table,
    tiles_ref,
    slot_ref,
    up_ref,
    down_ref,
    early,
    all_snap,
    mass_in,
    part_out,
    part_in,
    z_in,
    x_in,
    load_snap,
    load_rest,
    halo_send,
    halo_recv,
    snap_send,
    snap_recv,
    mass_send,
    mass_recv,
    part_send,
    part_recv,
    z_send,
    z_recv,
    x_send,
    x_recv,
):
    dom = lax.axis_index("dom")
    col = lax.axis_index("col")
    x_pos = dom // 16
    z_pos = (dom // 2) % 8
    core = dom % 2

    def col_peer(step):
        return (dom, lax.rem(col + step, COLS))

    def z_peer(step):
        return (x_pos * 16 + lax.rem(z_pos + step, 8) * 2 + core, col)

    def x_peer(step):
        return (lax.rem(x_pos + step, 4) * 16 + z_pos * 2 + core, col)

    sibling = dom + 1 - 2 * core

    upper = (lax.rem(dom + 1, 64), col)
    lower = (lax.rem(dom + 63, 64), col)

    snap_loads = [
        pltpu.make_async_copy(
            snap_hbm.at[:, :, pl.ds(block * BLOCK, BLOCK)], table.at[block], load_snap.at[block]
        )
        for block in range(OWN)
    ]
    name_loads = [
        pltpu.make_async_copy(up_hbm, up_ref, load_rest.at[0]),
        pltpu.make_async_copy(down_hbm, down_ref, load_rest.at[1]),
    ]
    tile_loads = [
        pltpu.make_async_copy(slot_hbm, slot_ref, load_rest.at[2]),
        pltpu.make_async_copy(tiles_hbm, tiles_ref, load_rest.at[3]),
    ]
    for load in name_loads + snap_loads + tile_loads:
        load.start()

    barrier = pltpu.get_barrier_semaphore()
    peers = [group(step) for group in (col_peer, z_peer) for step in FAR_FIRST]
    peers += [x_peer(step) for step in X_STEPS] + [(sibling, other) for other in range(COLS)] + [upper, lower]
    for peer in peers:
        pl.semaphore_signal(barrier, inc=1, device_id=peer, device_id_type=MESH)

    for load in name_loads + snap_loads:
        load.wait()
    for side, names in ((0, up_ref), (1, down_ref)):
        shared = pick(table, names[...], 0, OWN).astype(BF16)
        for half in range(2):
            for comp in range(3):
                table[BLOCKS + side * 2 + half, comp] = shared[
                    comp * SNAP : (comp + 1) * SNAP, half * BLOCK : (half + 1) * BLOCK
                ]

    def offset_of(step):
        return 4 + (1 - 2 * lax.rem(step, 2)) * lax.div(step + 1, 2)

    def chunk_of(step):
        return lax.rem(col + offset_of(step), COLS)

    def columns_of(chunk):
        return pl.ds(pl.multiple_of(chunk * BLOCK, BLOCK), BLOCK)

    def tile_sums(columns, total, own_values, first, count):
        coefs = [[tiles_ref[a, b, :, columns].astype(F32) for b in range(3)] for a in range(3)]
        if own_values is not None:
            for a in range(3):
                for b in range(3):
                    total[a] = total[a] + coefs[a][b][0:1] * own_values[b]
        slots = slot_ref[:, columns]
        for start in range(0, OTHERS, 2):
            ks = range(start, min(start + 2, OTHERS))
            found = pick(table, jnp.concatenate([slots[k : k + 1] for k in ks], axis=1), first, count)
            for place, k in enumerate(ks):
                for a in range(3):
                    for b in range(3):
                        values = found[b * SNAP : (b + 1) * SNAP, place * BLOCK : (place + 1) * BLOCK]
                        total[a] = total[a] + coefs[a][b][k + 1 : k + 2] * values
        return total

    def zeros():
        return [jnp.zeros((SNAP, BLOCK), F32) for _ in range(3)]

    def early_step(step, carry):
        chunk = chunk_of(step)
        total = tile_sums(columns_of(chunk), zeros(), table[chunk].astype(F32), 0, OWN)
        for a in range(3):
            early[step, a] = total[a]
        return carry

    for load in tile_loads:
        load.wait()
    def halo_copy(side):
        return pltpu.make_async_remote_copy(
            src_ref=table.at[pl.ds(BLOCKS + 2 * side, 2)],
            dst_ref=table.at[pl.ds(OWN + 2 * side, 2)],
            send_sem=halo_send.at[side],
            recv_sem=halo_recv.at[side],
            device_id=(upper, lower)[side],
            device_id_type=MESH,
        )

    def snap_copy(step):
        target = lax.rem(col + step, COLS)
        return pltpu.make_async_remote_copy(
            src_ref=table.at[target],
            dst_ref=all_snap.at[:, pl.ds(pl.multiple_of(col * SNAP, SNAP), SNAP), :],
            send_sem=snap_send.at[step - 1],
            recv_sem=snap_recv.at[step - 1],
            device_id=(dom, target),
            device_id_type=MESH,
        )

    def early_and_send(step, carry):
        early_step(step, carry)

        @pl.when(step == BEFORE - 1)
        def _():
            pl.semaphore_wait(barrier, len(peers))
            for side in range(2):
                halo_copy(side).start()
            for peer_step in FAR_FIRST:
                snap_copy(peer_step).start()
            all_snap[:, pl.ds(pl.multiple_of(col * SNAP, SNAP), SNAP), :] = table[col]

        return carry

    lax.fori_loop(0, EARLY, early_and_send, 0)

    for side in range(2):
        halo_copy(side).wait_recv()

    @pl.when(dom == 0)
    def _():
        table[OWN : OWN + 2] = jnp.zeros((2, 3, SNAP, BLOCK), BF16)

    @pl.when(dom == 63)
    def _():
        table[OWN + 2 : OWN + 4] = jnp.zeros((2, 3, SNAP, BLOCK), BF16)

    def mass_copy(step):
        chunk = chunk_of(step)
        return pltpu.make_async_remote_copy(
            src_ref=mass_ref.at[:, :, columns_of(chunk)],
            dst_ref=mass_in.at[step],
            send_sem=mass_send.at[step],
            recv_sem=mass_recv.at[step],
            device_id=(dom, chunk),
            device_id_type=MESH,
        )

    def part_copy(step, side, source):
        return pltpu.make_async_remote_copy(
            src_ref=part_out.at[step],
            dst_ref=part_in.at[source, step],
            send_sem=part_send.at[side, step],
            recv_sem=part_recv.at[source, step],
            device_id=((dom, sibling)[side], lax.rem(col + COLS - offset_of(step), COLS)),
            device_id_type=MESH,
        )

    def products(first, last):
        total = None
        for a in range(3):
            rows = mass_in[first:last, a].reshape((last - first) * SNAP, BLOCK)
            term = lax.dot_general(rows, all_snap[a], (((1,), (1,)), ((), ())), preferred_element_type=F32)
            total = term if total is None else total + term
        return total

    def finish(step, total):
        columns = columns_of(chunk_of(step))
        for a in range(3):
            mass_ref[a, :, columns] = total[a].astype(BF16)

        @pl.when(step < COLS - 1)
        def _():
            mass_copy(step).start()

    def answer(first, last, also_own):
        for step in range(first, last):
            mass_copy(step).wait_recv()
        total = products(first, last + 1 if also_own else last)
        for step in range(first, last):
            part_out[step] = total[(step - first) * SNAP : (step - first + 1) * SNAP]
            for side in range(2):
                part_copy(step, side, core).start()
        return total[(last - first) * SNAP :]

    def late_step(step, carry):
        columns = columns_of(chunk_of(step))
        total = tile_sums(columns, [early[step, a] for a in range(3)], None, OWN, BLOCKS - OWN)
        finish(step, total)
        return carry

    lax.fori_loop(0, EARLY, late_step, 0)

    def full_step(step, carry):
        chunk = chunk_of(step)
        total = tile_sums(columns_of(chunk), zeros(), table[chunk].astype(F32), 0, BLOCKS)
        finish(step, total)

        @pl.when(step == COLS - 2)
        def _():
            for peer_step in FAR_FIRST:
                snap_copy(peer_step).wait_recv()
            answer(0, FIRST_ANSWERS, False)

        return carry

    lax.fori_loop(EARLY, COLS, full_step, 0)

    mass_in[COLS - 1] = mass_ref[:, :, columns_of(col)]
    own_part = answer(FIRST_ANSWERS, COLS - 1, True)
    part_out[COLS - 1] = own_part
    part_copy(COLS - 1, 1, core).start()
    part_in[core, COLS - 1] = own_part
    for step in range(COLS - 1):
        part_copy(step, 0, core).wait_recv()
        part_copy(step, 1, 1 - core).wait_recv()
    part_copy(COLS - 1, 1, 1 - core).wait_recv()
    chip_part = part_in[0, 0]
    for place in range(1, 2 * COLS):
        chip_part = chip_part + part_in[place // COLS, place % COLS]

    def exchange(value, place, slots, steps, peer_of, sends, recvs):
        slots[place] = value
        copies = []
        for step in steps:
            copy = pltpu.make_async_remote_copy(
                src_ref=slots.at[place],
                dst_ref=slots.at[place],
                send_sem=sends.at[step - 1],
                recv_sem=recvs.at[step - 1],
                device_id=peer_of(step),
                device_id_type=MESH,
            )
            copy.start()
            copies.append(copy)
        for copy in copies:
            copy.wait_recv()
        total = slots[0]
        for other in range(1, len(steps) + 1):
            total = total + slots[other]
        return total, copies

    z_sum, z_copies = exchange(chip_part, z_pos, z_in, FAR_FIRST, z_peer, z_send, z_recv)
    x_sum, x_copies = exchange(z_sum, x_pos, x_in, X_STEPS, x_peer, x_send, x_recv)
    gram_ref[...] = x_sum / (3.0 * NODES * 64)

    for copy in z_copies + x_copies:
        copy.wait_send()
    for side in range(2):
        halo_copy(side).wait_send()
    for peer_step in FAR_FIRST:
        snap_copy(peer_step).wait_send()
    for step in range(COLS - 1):
        mass_copy(step).wait_send()
        part_copy(step, 0, core).wait_send()
        part_copy(step, 1, core).wait_send()
    part_copy(COLS - 1, 1, core).wait_send()


def body(snapshots, mass_tiles, tile_slot, send_up, send_down):
    vmem = pl.BlockSpec(memory_space=pltpu.VMEM)
    dma = pltpu.SemaphoreType.DMA
    mass, gram = pl.pallas_call(
        kernel,
        out_shape=(
            jax.ShapeDtypeStruct((3, SNAP, NODES), BF16),
            jax.ShapeDtypeStruct((SNAP, COLS * SNAP), F32),
        ),
        in_specs=[pl.BlockSpec(memory_space=pltpu.HBM)] * 5,
        out_specs=(vmem, vmem),
        scratch_shapes=[
            pltpu.VMEM((BLOCKS + 4, 3, SNAP, BLOCK), BF16),
            pltpu.VMEM((3, 3, OTHERS + 1, NODES), BF16),
            pltpu.VMEM((OTHERS, NODES), jnp.int32),
            pltpu.VMEM((1, 2 * BLOCK), jnp.int32),
            pltpu.VMEM((1, 2 * BLOCK), jnp.int32),
            pltpu.VMEM((EARLY, 3, SNAP, BLOCK), F32),
            pltpu.VMEM((3, COLS * SNAP, BLOCK), BF16),
            pltpu.VMEM((COLS, 3, SNAP, BLOCK), BF16),
            pltpu.VMEM((COLS, SNAP, COLS * SNAP), F32),
            pltpu.VMEM((2, COLS, SNAP, COLS * SNAP), F32),
            pltpu.VMEM((8, SNAP, COLS * SNAP), F32),
            pltpu.VMEM((4, SNAP, COLS * SNAP), F32),
            dma((OWN,)),
            dma((4,)),
            dma((2,)),
            dma((2,)),
        ]
        + [dma((7,))] * 4
        + [dma((2, COLS))] * 2
        + [dma((7,))] * 4,
        compiler_params=pltpu.CompilerParams(
            collective_id=0, has_side_effects=True, vmem_limit_bytes=32 * 2**20
        ),
        cost_estimate=pl.CostEstimate(flops=9_100_000_000, bytes_accessed=1_200_000, transcendentals=0),
    )(
        *(
            pltpu.with_memory_space_constraint(operand, pltpu.HBM)
            for operand in (
                jnp.transpose(snapshots, (1, 0, 2)),
                jnp.transpose(mass_tiles, (1, 2, 0, 3)),
                tile_slot,
                send_up.reshape(1, -1),
                send_down.reshape(1, -1),
            )
        )
    )
    return jnp.transpose(mass, (1, 0, 2)), jnp.transpose(gram, (1, 0))


def solution(mesh):
    placed = (P("col", None, "dom"), P(None, None, None, "dom"), P(None, "dom"), P("dom"), P("dom"))
    return jax.shard_map(
        body,
        mesh=mesh,
        in_specs=placed,
        out_specs=(P("col", None, "dom"), P(None, "col")),
        check_vma=False,
    )
```

```python
import functools

import jax
import jax.numpy as jnp
from jax import lax
from jax.experimental import pallas as pl
from jax.experimental.pallas import tpu as pltpu
from jax.sharding import PartitionSpec as P

BF16 = jnp.bfloat16
F32 = jnp.float32
MESH = pl.DeviceIdType.MESH

SNAP = 16
NODES = 2048
BLOCK = 256
OWN = NODES // BLOCK
BLOCKS = 12
OTHERS = 15
COLS = 8
BEFORE = 2
EARLY = 4
FAR_FIRST = (4, 3, 5, 2, 6, 1, 7)
X_STEPS = (2, 1, 3)
FIRST_ANSWERS = 5


def one_hot(low):
    rows = lax.broadcasted_iota(jnp.int16, (BLOCK, low.shape[1]), 0)
    return jnp.where(rows == low.astype(jnp.int16), jnp.array(1, BF16), jnp.array(0, BF16))


def pick(table, slots, first, count):
    low = slots & (BLOCK - 1)
    high = slots >> 8
    stacked = table[first : first + count].reshape(count * 3 * SNAP, BLOCK)
    products = jnp.dot(stacked, one_hot(low), preferred_element_type=F32)
    found = jnp.zeros((3 * SNAP, slots.shape[1]), F32)
    for block in range(count):
        rows = products[block * 3 * SNAP : (block + 1) * 3 * SNAP]
        found = jnp.where(high == first + block, rows, found)
    return found


def kernel(
    snap_hbm,
    tiles_hbm,
    slot_hbm,
    up_hbm,
    down_hbm,
    mass_ref,
    gram_ref,
    table,
    tiles_ref,
    slot_ref,
    up_ref,
    down_ref,
    early,
    all_snap,
    mass_in,
    part_out,
    part_in,
    z_in,
    x_in,
    load_snap,
    load_rest,
    halo_send,
    halo_recv,
    snap_send,
    snap_recv,
    mass_send,
    mass_recv,
    part_send,
    part_recv,
    z_send,
    z_recv,
    x_send,
    x_recv,
):
    dom = lax.axis_index("dom")
    col = lax.axis_index("col")
    x_pos = dom // 16
    z_pos = (dom // 2) % 8
    core = dom % 2

    def col_peer(step):
        return (dom, lax.rem(col + step, COLS))

    def z_peer(step):
        return (x_pos * 16 + lax.rem(z_pos + step, 8) * 2 + core, col)

    def x_peer(step):
        return (lax.rem(x_pos + step, 4) * 16 + z_pos * 2 + core, col)

    sibling = dom + 1 - 2 * core

    upper = (lax.rem(dom + 1, 64), col)
    lower = (lax.rem(dom + 63, 64), col)

    snap_loads = [
        pltpu.make_async_copy(
            snap_hbm.at[:, :, pl.ds(block * BLOCK, BLOCK)], table.at[block], load_snap.at[block]
        )
        for block in range(OWN)
    ]
    name_loads = [
        pltpu.make_async_copy(up_hbm, up_ref, load_rest.at[0]),
        pltpu.make_async_copy(down_hbm, down_ref, load_rest.at[1]),
    ]
    tile_loads = [
        pltpu.make_async_copy(slot_hbm, slot_ref, load_rest.at[2]),
        pltpu.make_async_copy(tiles_hbm, tiles_ref, load_rest.at[3]),
    ]
    for load in name_loads + snap_loads + tile_loads:
        load.start()

    barrier = pltpu.get_barrier_semaphore()
    peers = [group(step) for group in (col_peer, z_peer) for step in FAR_FIRST]
    peers += [x_peer(step) for step in X_STEPS] + [(sibling, other) for other in range(COLS)] + [upper, lower]
    for peer in peers:
        pl.semaphore_signal(barrier, inc=1, device_id=peer, device_id_type=MESH)

    for load in name_loads + snap_loads:
        load.wait()
    for side, names in ((0, up_ref), (1, down_ref)):
        shared = pick(table, names[...], 0, OWN).astype(BF16)
        for half in range(2):
            for comp in range(3):
                table[BLOCKS + side * 2 + half, comp] = shared[
                    comp * SNAP : (comp + 1) * SNAP, half * BLOCK : (half + 1) * BLOCK
                ]

    def offset_of(step):
        return 4 + (1 - 2 * lax.rem(step, 2)) * lax.div(step + 1, 2)

    def chunk_of(step):
        return lax.rem(col + offset_of(step), COLS)

    def columns_of(chunk):
        return pl.ds(pl.multiple_of(chunk * BLOCK, BLOCK), BLOCK)

    def tile_sums(columns, total, own_values, first, count):
        coefs = [[tiles_ref[a, b, :, columns].astype(F32) for b in range(3)] for a in range(3)]
        if own_values is not None:
            for a in range(3):
                for b in range(3):
                    total[a] = total[a] + coefs[a][b][0:1] * own_values[b]
        slots = slot_ref[:, columns]
        for start in range(0, OTHERS, 2):
            ks = range(start, min(start + 2, OTHERS))
            found = pick(table, jnp.concatenate([slots[k : k + 1] for k in ks], axis=1), first, count)
            for place, k in enumerate(ks):
                for a in range(3):
                    for b in range(3):
                        values = found[b * SNAP : (b + 1) * SNAP, place * BLOCK : (place + 1) * BLOCK]
                        total[a] = total[a] + coefs[a][b][k + 1 : k + 2] * values
        return total

    def zeros():
        return [jnp.zeros((SNAP, BLOCK), F32) for _ in range(3)]

    def early_step(step, carry):
        chunk = chunk_of(step)
        total = tile_sums(columns_of(chunk), zeros(), table[chunk].astype(F32), 0, OWN)
        for a in range(3):
            early[step, a] = total[a]
        return carry

    for load in tile_loads:
        load.wait()
    def halo_copy(side):
        return pltpu.make_async_remote_copy(
            src_ref=table.at[pl.ds(BLOCKS + 2 * side, 2)],
            dst_ref=table.at[pl.ds(OWN + 2 * side, 2)],
            send_sem=halo_send.at[side],
            recv_sem=halo_recv.at[side],
            device_id=(upper, lower)[side],
            device_id_type=MESH,
        )

    def snap_copy(step):
        target = lax.rem(col + step, COLS)
        return pltpu.make_async_remote_copy(
            src_ref=table.at[target],
            dst_ref=all_snap.at[:, pl.ds(pl.multiple_of(col * SNAP, SNAP), SNAP), :],
            send_sem=snap_send.at[step - 1],
            recv_sem=snap_recv.at[step - 1],
            device_id=(dom, target),
            device_id_type=MESH,
        )

    def early_and_send(step, carry):
        early_step(step, carry)

        @pl.when(step == BEFORE - 1)
        def _():
            pl.semaphore_wait(barrier, len(peers))
            for side in range(2):
                halo_copy(side).start()
            for peer_step in FAR_FIRST:
                snap_copy(peer_step).start()
            all_snap[:, pl.ds(pl.multiple_of(col * SNAP, SNAP), SNAP), :] = table[col]

        return carry

    lax.fori_loop(0, EARLY, early_and_send, 0)

    for side in range(2):
        halo_copy(side).wait_recv()

    @pl.when(dom == 0)
    def _():
        table[OWN : OWN + 2] = jnp.zeros((2, 3, SNAP, BLOCK), BF16)

    @pl.when(dom == 63)
    def _():
        table[OWN + 2 : OWN + 4] = jnp.zeros((2, 3, SNAP, BLOCK), BF16)

    def mass_copy(step):
        chunk = chunk_of(step)
        return pltpu.make_async_remote_copy(
            src_ref=mass_ref.at[:, :, columns_of(chunk)],
            dst_ref=mass_in.at[step],
            send_sem=mass_send.at[step],
            recv_sem=mass_recv.at[step],
            device_id=(dom, chunk),
            device_id_type=MESH,
        )

    def part_copy(step, side, source):
        return pltpu.make_async_remote_copy(
            src_ref=part_out.at[step],
            dst_ref=part_in.at[source, step],
            send_sem=part_send.at[side, step],
            recv_sem=part_recv.at[source, step],
            device_id=((dom, sibling)[side], lax.rem(col + COLS - offset_of(step), COLS)),
            device_id_type=MESH,
        )

    def products(first, last):
        total = None
        for a in range(3):
            rows = mass_in[first:last, a].reshape((last - first) * SNAP, BLOCK)
            term = lax.dot_general(rows, all_snap[a], (((1,), (1,)), ((), ())), preferred_element_type=F32)
            total = term if total is None else total + term
        return total

    def finish(step, total):
        columns = columns_of(chunk_of(step))
        for a in range(3):
            mass_ref[a, :, columns] = total[a].astype(BF16)

        @pl.when(step < COLS - 1)
        def _():
            mass_copy(step).start()

    def answer(first, last, also_own):
        for step in range(first, last):
            mass_copy(step).wait_recv()
        total = products(first, last + 1 if also_own else last)
        for step in range(first, last):
            part_out[step] = total[(step - first) * SNAP : (step - first + 1) * SNAP]
            for side in (1, 0):
                part_copy(step, side, core).start()
        return total[(last - first) * SNAP :]

    def late_step(step, carry):
        columns = columns_of(chunk_of(step))
        total = tile_sums(columns, [early[step, a] for a in range(3)], None, OWN, BLOCKS - OWN)
        finish(step, total)
        return carry

    lax.fori_loop(0, EARLY, late_step, 0)

    def full_step(step, carry):
        chunk = chunk_of(step)
        total = tile_sums(columns_of(chunk), zeros(), table[chunk].astype(F32), 0, BLOCKS)
        finish(step, total)

        @pl.when(step == COLS - 2)
        def _():
            for peer_step in FAR_FIRST:
                snap_copy(peer_step).wait_recv()
            answer(0, FIRST_ANSWERS, False)

        return carry

    lax.fori_loop(EARLY, COLS, full_step, 0)

    mass_in[COLS - 1] = mass_ref[:, :, columns_of(col)]
    own_part = answer(FIRST_ANSWERS, COLS - 1, True)
    part_out[COLS - 1] = own_part
    part_copy(COLS - 1, 1, core).start()
    part_in[core, COLS - 1] = own_part
    for step in range(COLS - 1):
        part_copy(step, 0, core).wait_recv()
        part_copy(step, 1, 1 - core).wait_recv()
    part_copy(COLS - 1, 1, 1 - core).wait_recv()
    chip_part = part_in[0, 0]
    for place in range(1, 2 * COLS):
        chip_part = chip_part + part_in[place // COLS, place % COLS]

    def exchange(value, place, slots, steps, peer_of, sends, recvs):
        slots[place] = value
        copies = []
        for step in steps:
            copy = pltpu.make_async_remote_copy(
                src_ref=slots.at[place],
                dst_ref=slots.at[place],
                send_sem=sends.at[step - 1],
                recv_sem=recvs.at[step - 1],
                device_id=peer_of(step),
                device_id_type=MESH,
            )
            copy.start()
            copies.append(copy)
        for copy in copies:
            copy.wait_recv()
        total = slots[0]
        for other in range(1, len(steps) + 1):
            total = total + slots[other]
        return total, copies

    x_sum, x_copies = exchange(chip_part, x_pos, x_in, X_STEPS, x_peer, x_send, x_recv)
    z_sum, z_copies = exchange(x_sum, z_pos, z_in, FAR_FIRST, z_peer, z_send, z_recv)
    gram_ref[...] = z_sum / (3.0 * NODES * 64)

    for copy in z_copies + x_copies:
        copy.wait_send()
    for side in range(2):
        halo_copy(side).wait_send()
    for peer_step in FAR_FIRST:
        snap_copy(peer_step).wait_send()
    for step in range(COLS - 1):
        mass_copy(step).wait_send()
        part_copy(step, 0, core).wait_send()
        part_copy(step, 1, core).wait_send()
    part_copy(COLS - 1, 1, core).wait_send()


def body(snapshots, mass_tiles, tile_slot, send_up, send_down):
    vmem = pl.BlockSpec(memory_space=pltpu.VMEM)
    dma = pltpu.SemaphoreType.DMA
    mass, gram = pl.pallas_call(
        kernel,
        out_shape=(
            jax.ShapeDtypeStruct((3, SNAP, NODES), BF16),
            jax.ShapeDtypeStruct((SNAP, COLS * SNAP), F32),
        ),
        in_specs=[pl.BlockSpec(memory_space=pltpu.HBM)] * 5,
        out_specs=(vmem, vmem),
        scratch_shapes=[
            pltpu.VMEM((BLOCKS + 4, 3, SNAP, BLOCK), BF16),
            pltpu.VMEM((3, 3, OTHERS + 1, NODES), BF16),
            pltpu.VMEM((OTHERS, NODES), jnp.int32),
            pltpu.VMEM((1, 2 * BLOCK), jnp.int32),
            pltpu.VMEM((1, 2 * BLOCK), jnp.int32),
            pltpu.VMEM((EARLY, 3, SNAP, BLOCK), F32),
            pltpu.VMEM((3, COLS * SNAP, BLOCK), BF16),
            pltpu.VMEM((COLS, 3, SNAP, BLOCK), BF16),
            pltpu.VMEM((COLS, SNAP, COLS * SNAP), F32),
            pltpu.VMEM((2, COLS, SNAP, COLS * SNAP), F32),
            pltpu.VMEM((8, SNAP, COLS * SNAP), F32),
            pltpu.VMEM((4, SNAP, COLS * SNAP), F32),
            dma((OWN,)),
            dma((4,)),
            dma((2,)),
            dma((2,)),
        ]
        + [dma((7,))] * 4
        + [dma((2, COLS))] * 2
        + [dma((7,))] * 4,
        compiler_params=pltpu.CompilerParams(
            collective_id=0, has_side_effects=True, vmem_limit_bytes=32 * 2**20
        ),
        cost_estimate=pl.CostEstimate(flops=9_100_000_000, bytes_accessed=1_200_000, transcendentals=0),
    )(
        *(
            pltpu.with_memory_space_constraint(operand, pltpu.HBM)
            for operand in (
                jnp.transpose(snapshots, (1, 0, 2)),
                jnp.transpose(mass_tiles, (1, 2, 0, 3)),
                tile_slot,
                send_up.reshape(1, -1),
                send_down.reshape(1, -1),
            )
        )
    )
    return jnp.transpose(mass, (1, 0, 2)), jnp.transpose(gram, (1, 0))


def solution(mesh):
    placed = (P("col", None, "dom"), P(None, None, None, "dom"), P(None, "dom"), P("dom"), P("dom"))
    return jax.shard_map(
        body,
        mesh=mesh,
        in_specs=placed,
        out_specs=(P("col", None, "dom"), P(None, "col")),
        check_vma=False,
    )
```
